128 devices in a mesh: band: 16 (over x_hi, y, core), slab: 8 (over z, x_lo).
Axes of the slice: x: 4 (x_hi: 2, x_lo: 2; x = x_hi * 2 + x_lo), y: 4, z: 4, core: 2. Of those that a mesh axis runs over, the one named last changes fastest.
Arguments:
- orbitals: float32 [32, 72, 72, 72], P('band', 'slab'), may hold values from -5 to 5
- occupation: float32 [32], P('band'), may hold values from 0.3 to 1
Outputs:
- exchange_field: float32 [32, 72, 72, 72], P('band', 'slab')
The draws below stay inside these ranges and needn't reach their ends.
All inputs are finite; a program needn't handle non-finite values.
Results may differ from the reference program's by a relative error of at most 0.0084.
Values may be sent and summed in bfloat16 or wider, within the bound.
A program may use at most 128 MiB of HBM per device.

```python
import math
import jax
import jax.numpy as jnp
from jax import lax

NG = 72
NORB = 32


def draw_orbitals(key, part):
    key = jax.random.fold_in(key, 11)
    normal_part = jax.random.normal(key, (NORB, NG, NG, NG), jnp.float32)
    return jnp.clip(normal_part, -5.0, 5.0)


def shard_levels(key, dims, split, low, high):
    gain, own = 1.0, jax.random.fold_in(key, 6)
    for dim, parts in split:
        steps = jnp.exp(jax.random.uniform(jax.random.fold_in(own, dim), (parts,), jnp.float32, low / len(split), high / len(split)))
        gain = gain * jnp.repeat(steps, dims[dim] // parts).reshape([-1 if axis == dim else 1 for axis in range(len(dims))])
    return gain


def setup_inputs(seed: int = 0) -> dict:
    key_of = jax.random.split(jax.random.key(seed), 3)
    orbitals = draw_orbitals(jax.random.fold_in(key_of[2], 71), 0)
    occupation = jnp.clip(0.3 + 0.7 * jax.random.uniform(key_of[1], (NORB,), jnp.float32) ** shard_levels(key_of[1], (NORB,), ((0, 16),), -0.2, 0.2), 0.3, 1.0)
    return {"orbitals": orbitals, "occupation": occupation}


BOX_LENGTH = 37.25
PRECISE = lax.Precision.HIGHEST

def hartley_table(count):
    positions = jnp.arange(count, dtype=jnp.int32)
    products = positions[:, None] * positions[None, :] % count
    angles = products.astype(jnp.float32) * (2.0 * math.pi / count)
    return jnp.cos(angles) + jnp.sin(angles)

def wave_square(positions, count):
    signed = jnp.where(positions < count // 2, positions, positions - count)
    return (signed * signed).astype(jnp.float32)

def coulomb_kernel(along_x, along_y, along_z):
    summed = along_x[:, None, None] + along_y[None, :, None] + along_z[None, None, :]
    factor = (2.0 * math.pi / BOX_LENGTH) ** 2
    denominator = jnp.where(summed > 0.0, summed, 1.0)
    return jnp.where(summed > 0.0, 4.0 * math.pi / factor / denominator, 0.0)

def forward_planes(density, cas_table):
    halfway = jnp.einsum('pxyz,zk->pxyk', density, cas_table, precision=PRECISE)
    return jnp.einsum('pxyk,yj->pxjk', halfway, cas_table, precision=PRECISE)

def reference(orbitals, occupation):
    cas_table = hartley_table(NG)
    rounded_table = lax.optimization_barrier(cas_table.astype(jnp.bfloat16)).astype(jnp.float32)
    squares = wave_square(jnp.arange(NG, dtype=jnp.int32), NG)
    kernel = coulomb_kernel(squares, squares, squares)
    volume = float(NG ** 3)

    def one_orbital(position):
        chosen = lax.dynamic_index_in_dim(orbitals, position, 0, keepdims=True)
        density = chosen * orbitals
        planes = forward_planes(density, cas_table).astype(jnp.bfloat16)
        planes = lax.optimization_barrier(planes)
        spectrum = jnp.einsum('pxyz,xi->piyz', planes.astype(jnp.float32), rounded_table, precision=PRECISE) * kernel
        returned = jnp.einsum('piyz,xi->pxyz', spectrum, cas_table, precision=PRECISE).astype(jnp.bfloat16)
        returned = lax.optimization_barrier(returned)
        halfway = jnp.einsum('pxjk,yj->pxyk', returned.astype(jnp.float32), rounded_table, precision=PRECISE)
        potential = jnp.einsum('pxyk,zk->pxyz', halfway, cas_table, precision=PRECISE) / volume
        return jnp.einsum('j,jxyz->xyz', occupation, orbitals * potential, precision=PRECISE)
    summed = lax.map(one_orbital, jnp.arange(NORB, dtype=jnp.int32))
    return -1.0 / math.sqrt(NORB) * summed
```

```python
import math

import jax
import jax.numpy as jnp
import numpy as np
from jax import lax
from jax.experimental import pallas as pl
from jax.experimental.pallas import tpu as pltpu

N = 72
BOX_LENGTH = 37.25
ROWS, USED, LANES = 224, 216, 256
F32, BF16 = jnp.float32, jnp.bfloat16
MESH = pl.DeviceIdType.MESH
BLOCK = 24


def tables():
    positions = np.arange(N)
    angles = (positions[:, None] * positions[None, :] % N) * (2.0 * math.pi / N)
    cas = np.cos(angles) + np.sin(angles)
    spread = np.zeros((LANES, 384), np.float32)
    gather = np.zeros((384, LANES), np.float32)
    for part in range(3):
        spread[72 * part : 72 * part + 72, 128 * part : 128 * part + 72] = cas
        gather[128 * part : 128 * part + 72, 72 * part : 72 * part + 72] = cas
    squares = np.where(positions < N // 2, positions, positions - N).astype(np.float64) ** 2
    summed = squares[:, None, None] + squares[None, :, None] + squares[None, None, :]
    scale = 4.0 * math.pi / (2.0 * math.pi / BOX_LENGTH) ** 2 * (-1.0 / math.sqrt(32.0) / N**3)
    coulomb = np.zeros((N, N, 128), np.float32)
    coulomb[:, :, :N] = np.where(summed > 0, scale / np.where(summed > 0, summed, 1.0), 0.0)
    short = lambda value: jnp.asarray(value, F32).astype(BF16)
    return short(spread), short(cas), short(gather), jnp.asarray(coulomb)


class Place:
    def __init__(self):
        band, slab = lax.axis_index("band"), lax.axis_index("slab")
        xh, y, k = band // 8, band // 2 % 4, band % 2
        z, xl = slab // 2, slab % 2
        self.slab, self.z, self.y, self.k = slab, z, y, k
        group = xh * 4 + y
        w = (xh + xl) % 2
        column = w * 4 + z

        def swapped(of, against):
            return (of - against + 8) // 8

        kk = (k + swapped(group, column)) % 2
        far = group - column + 8
        self.diagonal = (far // 8) * ((16 - far) // 8)

        def member(xh2, xl2, y2):
            core = (kk + swapped(xh2 * 4 + y2, column)) % 2
            return (xh2 * 8 + y2 * 2 + core, 2 * z + xl2)

        self.row_x = (band, 2 * z + 1 - xl)
        self.row_ring = ((band, 2 * ((z + 1) % 4) + xl), (band, 2 * ((z + 3) % 4) + xl))
        self.col_x = member(1 - xh, 1 - xl, y)
        self.col_ring = (member(xh, xl, (y + 1) % 4), member(xh, xl, (y + 3) % 4))
        xh2 = (xh + xl + 1) % 2
        core = (k + swapped(xh2 * 4 + z, group)) % 2
        self.turn = (xh2 * 8 + z * 2 + core, 2 * y + 1 - xl)
        self.back = (w * 8 + z * 2 + kk, 2 * y + 1 - xl)
        self.row_slab = lambda step, line: 2 * ((z + step) % 4) + (1 - xl if line else xl)
        self.col_slab = lambda step, line: 2 * ((y + step) % 4) + (xl if line else 1 - xl)
        d = (y - z + 4) % 4
        half, last = d // 2, d // 3
        self.order = (half - last, 1 + 2 * half, 2 - 2 * half + last, 3 - half)

    def partners(self):
        return (self.row_x, *self.row_ring, self.col_x, *self.col_ring, self.turn, self.back)

    def pair(self, p):
        d, k = self.diagonal, self.k
        i = (1 - d) * (p // 2 if p < 4 else 0) + d * (0, 0, 1, 0, 1)[p]
        j = (1 - d) * (2 + p % 2) + d * ((0, 1, 1, 2, 3)[p] + (0, 0, 0, 1, -1)[p] * k)
        return i, j


def forward(orb, w, spread, cas, i, j, s, p):
    density = orb[i // 2, s, i % 2] * orb[j // 2, s, j % 2]
    h = jnp.dot(density, spread[...], preferred_element_type=F32)
    columns = [
        jnp.concatenate([h[24 * x : 24 * x + 24, 128 * t : 128 * t + 128] for t in range(3)], axis=0)
        for x in range(9)
    ]
    planes = jnp.dot(
        cas[...], jnp.concatenate(columns, axis=1).astype(BF16), preferred_element_type=F32
    )
    for x in range(9):
        w[p, pl.ds(pl.multiple_of(s * 648 + 72 * x, 8), 72), :] = planes[:, 128 * x : 128 * x + 128]


def middle(w, cas, coulomb, p, b):
    rows = [w[p, pl.ds(b + t, 72, stride=72), :] for t in range(BLOCK)]
    spectrum = jnp.dot(
        cas[...], jnp.concatenate(rows, axis=1).astype(BF16), preferred_element_type=F32
    )
    filtered = [spectrum[:, 128 * t : 128 * t + 128] * coulomb[b + t] for t in range(BLOCK)]
    back = jnp.dot(
        cas[...], jnp.concatenate(filtered, axis=1).astype(BF16), preferred_element_type=F32
    )
    for t in range(BLOCK):
        w[p, pl.ds(b + t, 72, stride=72), :] = back[:, 128 * t : 128 * t + 128]


def backward(orb, w, field, gather, cas, i, j, s, p):
    columns = [w[p, pl.ds(pl.multiple_of(s * 648 + 72 * x, 8), 72), :] for x in range(9)]
    half = jnp.dot(
        cas[...], jnp.concatenate(columns, axis=1).astype(BF16), preferred_element_type=F32
    )
    rows = [
        jnp.concatenate([half[24 * t : 24 * t + 24, 128 * x : 128 * x + 128] for t in range(3)], axis=1)
        for x in range(9)
    ]
    potential = jnp.dot(
        jnp.concatenate(rows, axis=0).astype(BF16), gather[...], preferred_element_type=F32
    )
    for target, source, weight in ((i, j, False), (j, i, True)):
        occupation = orb[source // 2, s, source % 2, 216:218].astype(F32)
        occupation = occupation[0:1] + occupation[1:2]
        if weight:
            occupation = occupation * jnp.where(i == j, 0.0, 1.0)
        term = (orb[source // 2, s, source % 2, 0:USED].astype(F32) * occupation) * potential
        field[target] = field[target] + term


def pack(value, occupation):
    parts = [
        jnp.concatenate([value[x, 24 * t : 24 * t + 24, :] for t in range(3)], axis=1) for x in range(9)
    ]
    body = jnp.concatenate(parts, axis=0)
    body = jnp.concatenate([body, jnp.zeros((USED, LANES - 216), F32)], axis=1)
    whole = jnp.full((8, LANES), occupation, F32)
    high = whole.astype(BF16).astype(F32)
    row = lax.broadcasted_iota(jnp.int32, (8, LANES), 0)
    tail = jnp.where(row == 0, high, jnp.where(row == 1, whole - high, 0.0))
    return jnp.concatenate([body, tail], axis=0).astype(BF16)


def kernel(
    mine, occupation, spread, cas, gather, coulomb_hbm, out,
    orb, w, field, part, land_half, land_ring, land_x, land_turn, coulomb, send_sem, recv_sem, copy_sem,
):
    me = Place()

    def remote(source, target, index, device):
        return pltpu.make_async_remote_copy(
            src_ref=source,
            dst_ref=target,
            send_sem=send_sem.at[index],
            recv_sem=recv_sem.at[index],
            device_id=device,
            device_id_type=MESH,
        )

    barrier = pltpu.get_barrier_semaphore()
    for device in me.partners():
        pl.semaphore_signal(barrier, inc=1, device_id=device, device_id_type=MESH)
    table = pltpu.make_async_copy(coulomb_hbm, coulomb, copy_sem)
    table.start()
    for o in range(2):
        orb[0, me.slab, o] = pack(mine[o], occupation[o])
    pl.semaphore_wait(barrier, len(me.partners()))

    sides = (
        (0, 0, me.row_slab, me.row_x, me.row_ring),
        (1, 9, me.col_slab, me.col_x, me.col_ring),
    )
    started = []

    def start(*copy):
        copy = remote(*copy)
        copy.start()
        started.append(copy)
        return copy

    def own(side):
        ab, base, slab, x, ring = side
        piece = orb.at[ab, slab(0, 0)]
        return [start(piece, piece, base + n, device) for n, device in enumerate((ring[0], ring[1], x))]

    def pass_x(side):
        ab, base, slab, _, ring = side
        piece = orb.at[ab, slab(0, 1)]
        return [start(piece, piece, base + 3 + n, ring[n]) for n in range(2)]

    def pass_half(side, line):
        ab, base, slab, _, ring = side
        pieces = [orb.at[ab, slab(3, line), 0], orb.at[ab, slab(1, line), 1]]
        return [start(pieces[n], pieces[n], base + 5 + 2 * line + n, ring[n]) for n in range(2)]

    row, col = sides
    origin = orb.at[0, me.slab]
    turned = start(origin, orb.at[1, me.slab], 18, me.turn)
    row_own = own(row)
    row_own[2].wait_recv()
    row_x = pass_x(row)
    turned.wait_recv()
    col_own = own(col)
    row_own[0].wait_recv()
    row_own[1].wait_recv()
    row_halves = pass_half(row, 0)
    col_own[2].wait_recv()
    col_x = pass_x(col)
    row_x[0].wait_recv()
    row_x[1].wait_recv()
    row_halves += pass_half(row, 1)
    col_own[0].wait_recv()
    col_own[1].wait_recv()
    col_halves = pass_half(col, 0)
    col_x[0].wait_recv()
    col_x[1].wait_recv()
    col_halves += pass_half(col, 1)

    def slab_of(first, t):
        step = me.order[first] + (me.order[first + 1] - me.order[first]) * (t // 2)
        return 2 * ((me.z + step) % 4) + t % 2

    def spectra(first):
        def body(t, _):
            s = slab_of(first, t)
            for p in range(4):
                i, j = me.pair(p)
                forward(orb, w, spread, cas, i, j, s, p)
            return 0

        lax.fori_loop(0, 4, body, 0)

    spectra(0)
    for copy in row_halves + col_halves:
        copy.wait_recv()
    spectra(2)

    @pl.when(me.diagonal == 1)
    def _():
        def body(s, _):
            i, j = me.pair(4)
            forward(orb, w, spread, cas, i, j, s, 4)
            return 0

        lax.fori_loop(0, 8, body, 0)

    table.wait()

    def solve(t, _):
        middle(w, cas, coulomb, t // (N // BLOCK), t % (N // BLOCK) * BLOCK)
        return 0

    lax.fori_loop(0, (4 + me.diagonal) * (N // BLOCK), solve, 0)

    def fields(first):
        def body(t, _):
            s = slab_of(first, t)
            field[...] = jnp.zeros_like(field)
            for p in range(4):
                i, j = me.pair(p)
                backward(orb, w, field, gather, cas, i, j, s, p)

            @pl.when(me.diagonal == 1)
            def _():
                i, j = me.pair(4)
                backward(orb, w, field, gather, cas, i, j, s, 4)

            for o in range(4):
                whole = jnp.concatenate([field[o], jnp.zeros((ROWS - USED, LANES), F32)], axis=0)
                part[o // 2, s, o % 2] = whole.astype(BF16)
            return 0

        lax.fori_loop(0, 4, body, 0)

    def add(*values):
        return sum((value.astype(F32) for value in values[1:]), values[0].astype(F32))

    fields(2)
    halves = {}
    for ab, base, slab, _, ring in sides:
        for line in (1, 0):
            for n in range(2):
                halves[ab, line, n] = start(
                    part.at[ab, slab(2, line), n],
                    land_half.at[ab, n, line],
                    19 + base + 2 * line + n,
                    ring[n],
                )
    fields(0)
    rings = {}
    for line in (1, 0):
        for n in range(2):
            for ab, base, slab, _, ring in sides:
                halves[ab, line, n].wait_recv()
                s = slab((1, 3)[n], line)
                part[ab, s, n] = add(part[ab, s, n], land_half[ab, n, line]).astype(BF16)
                rings[ab, line, n] = start(
                    part.at[ab, s], land_ring.at[ab, n, line], 23 + base + 2 * line + n, ring[n]
                )
    across = {}
    for ab, base, slab, x, _ in sides:
        rings[ab, 1, 0].wait_recv()
        rings[ab, 1, 1].wait_recv()
        s = slab(0, 1)
        part[ab, s] = add(part[ab, s], land_ring[ab, 0, 1], land_ring[ab, 1, 1]).astype(BF16)
        across[ab] = start(part.at[ab, s], land_x.at[ab], 27 + base, x)
    totals = {}
    for ab, base, slab, x, _ in (col, row):
        rings[ab, 0, 0].wait_recv()
        rings[ab, 0, 1].wait_recv()
        across[ab].wait_recv()
        s = slab(0, 0)
        part[ab, s] = add(
            part[ab, s], land_ring[ab, 0, 0], land_ring[ab, 1, 0], land_x[ab]
        ).astype(BF16)
        if ab == 1:
            turned_back = start(part.at[1, s], land_turn, 37, me.back)
    turned_back.wait_recv()
    s = me.row_slab(0, 0)
    for o in range(2):
        total = add(part[0, s, o], land_turn[o])
        for x in range(9):
            for t in range(3):
                out[o, x, 24 * t : 24 * t + 24, :] = total[24 * x : 24 * x + 24, 72 * t : 72 * t + 72]
    for copy in started:
        copy.wait_send()


def on_device(orbitals, occupation):
    vmem = pl.BlockSpec(memory_space=pltpu.VMEM)
    piece = (2, ROWS, LANES)
    return pl.pallas_call(
        kernel,
        out_shape=jax.ShapeDtypeStruct(orbitals.shape, F32),
        in_specs=[vmem, pl.BlockSpec(memory_space=pltpu.SMEM), vmem, vmem, vmem, pl.BlockSpec(memory_space=pl.ANY)],
        out_specs=vmem,
        scratch_shapes=[
            pltpu.VMEM((2, 8, *piece), BF16),
            pltpu.VMEM((5, N * N, 128), F32),
            pltpu.VMEM((4, USED, LANES), F32),
            pltpu.VMEM((2, 8, *piece), BF16),
            pltpu.VMEM((2, 2, 2, ROWS, LANES), BF16),
            pltpu.VMEM((2, 2, 2, *piece), BF16),
            pltpu.VMEM((2, *piece), BF16),
            pltpu.VMEM(piece, BF16),
            pltpu.VMEM((N, N, 128), F32),
            pltpu.SemaphoreType.DMA((38,)),
            pltpu.SemaphoreType.DMA((38,)),
            pltpu.SemaphoreType.DMA,
        ],
        compiler_params=pltpu.CompilerParams(
            collective_id=0, has_side_effects=True, vmem_limit_bytes=56 * 2**20
        ),
        name="exchange",
    )(orbitals, occupation, *tables())


def solution(mesh):
    return jax.shard_map(
        on_device,
        mesh=mesh,
        in_specs=(jax.sharding.PartitionSpec("band", "slab", None, None), jax.sharding.PartitionSpec("band")),
        out_specs=jax.sharding.PartitionSpec("band", "slab", None, None),
        check_vma=False,
    )
```

```python
import math

import jax
import jax.numpy as jnp
import numpy as np
from jax import lax
from jax.experimental import pallas as pl
from jax.experimental.pallas import tpu as pltpu

N = 72
BOX_LENGTH = 37.25
ROWS, LANES, LINES = 96, 512, 648
F32, BF16 = jnp.float32, jnp.bfloat16
MESH = pl.DeviceIdType.MESH
BLOCK = 24


def tables():
    positions = np.arange(N)
    angles = (positions[:, None] * positions[None, :] % N) * (2.0 * math.pi / N)
    cas = np.cos(angles) + np.sin(angles)
    spread = np.zeros((4, 256, 256), np.float32)
    gather = np.zeros((4, 256, 256), np.float32)
    for block in range(7):
        window, lane = block // 2, 72 * block - 128 * (block // 2)
        column = 128 * (block % 2)
        spread[window, lane : lane + 72, column : column + 72] = cas
        gather[window, column : column + 72, lane : lane + 72] = cas
    squares = np.where(positions < N // 2, positions, positions - N).astype(np.float64) ** 2
    summed = squares[:, None, None] + squares[None, :, None] + squares[None, None, :]
    scale = 4.0 * math.pi / (2.0 * math.pi / BOX_LENGTH) ** 2 * (-1.0 / math.sqrt(32.0) / N**3)
    coulomb = np.zeros((N, N, 128), np.float32)
    coulomb[:, :, :N] = np.where(summed > 0, scale / np.where(summed > 0, summed, 1.0), 0.0)
    short = lambda value: jnp.asarray(value, F32).astype(BF16)
    return short(spread), short(cas), short(gather), jnp.asarray(coulomb)


class Place:
    def __init__(self):
        band, slab = lax.axis_index("band"), lax.axis_index("slab")
        xh, y, k = band // 8, band // 2 % 4, band % 2
        z, xl = slab // 2, slab % 2
        self.slab, self.z, self.y, self.k = slab, z, y, k
        group = xh * 4 + y
        w = (xh + xl) % 2
        column = w * 4 + z

        def swapped(of, against):
            return (of - against + 8) // 8

        kk = (k + swapped(group, column)) % 2
        far = group - column + 8
        self.diagonal = (far // 8) * ((16 - far) // 8)

        def member(xh2, xl2, y2):
            core = (kk + swapped(xh2 * 4 + y2, column)) % 2
            return (xh2 * 8 + y2 * 2 + core, 2 * z + xl2)

        self.row_x = (band, 2 * z + 1 - xl)
        self.row_ring = ((band, 2 * ((z + 1) % 4) + xl), (band, 2 * ((z + 3) % 4) + xl))
        self.col_x = member(1 - xh, 1 - xl, y)
        self.col_ring = (member(xh, xl, (y + 1) % 4), member(xh, xl, (y + 3) % 4))
        xh2 = (xh + xl + 1) % 2
        y2 = (2 * y - z + 4) % 4
        core = (k + swapped(xh2 * 4 + y2, group)) % 2
        self.turn = (xh2 * 8 + y2 * 2 + core, 2 * y + 1 - xl)
        self.back = (w * 8 + z * 2 + kk, 2 * ((2 * z - y + 4) % 4) + 1 - xl)
        self.row_slab = lambda step, line: 2 * ((z + step) % 4) + (1 - xl if line else xl)
        self.col_slab = lambda step, line: 2 * ((2 * z - y - step + 8) % 4) + (xl if line else 1 - xl)
        d = (z - y + 4) % 4
        half, last, some = d // 2, d // 3, (d + 2) // 3
        self.way_in = (half - last, 1 + 2 * half, 2 - 2 * half + last, 3 - half)
        self.way_out = ((d + 2) % 4, 1 + some, 3 - 3 * some + half - last, d + half - last)

    def partners(self):
        return (self.row_x, *self.row_ring, self.col_x, *self.col_ring, self.turn, self.back)

    def pair(self, p):
        d, k = self.diagonal, self.k
        i = (1 - d) * (p // 2 if p < 4 else 0) + d * (0, 0, 1, 0, 1)[p]
        j = (1 - d) * (2 + p % 2) + d * ((0, 1, 1, 2, 3)[p] + (0, 0, 0, 1, -1)[p] * k)
        return i, j


def lines_of(blocks, first, count):
    pieces = []
    while count:
        block, row = first // ROWS, first % ROWS
        size = min(count, ROWS - row)
        pieces.append(blocks[block][row : row + size])
        first, count = first + size, count - size
    return pieces[0] if len(pieces) == 1 else jnp.concatenate(pieces, axis=0)


def forward(orb, w, spread, cas, i, j, s, p):
    density = orb[i // 2, s, i % 2] * orb[j // 2, s, j % 2]
    blocks = []
    for t in range(3):
        h = jnp.dot(density[:, 128 * t : 128 * t + 256], spread[t], preferred_element_type=F32)
        blocks += [h[:, 0:128], h[:, 128:256]]
    blocks.append(jnp.dot(density[:, 384:512], spread[3, 0:128, 0:128], preferred_element_type=F32))
    columns = [lines_of(blocks, 72 * x, 72) for x in range(9)]
    planes = jnp.dot(
        cas[...], jnp.concatenate(columns, axis=1).astype(BF16), preferred_element_type=F32
    )
    for x in range(9):
        w[p, pl.ds(pl.multiple_of(s * LINES + 72 * x, 8), 72), :] = planes[:, 128 * x : 128 * x + 128]


def middle(w, cas, coulomb, p, b):
    rows = [w[p, pl.ds(b + t, 72, stride=72), :] for t in range(BLOCK)]
    spectrum = jnp.dot(
        cas[...], jnp.concatenate(rows, axis=1).astype(BF16), preferred_element_type=F32
    )
    filtered = [spectrum[:, 128 * t : 128 * t + 128] * coulomb[b + t] for t in range(BLOCK)]
    back = jnp.dot(
        cas[...], jnp.concatenate(filtered, axis=1).astype(BF16), preferred_element_type=F32
    )
    for t in range(BLOCK):
        w[p, pl.ds(b + t, 72, stride=72), :] = back[:, 128 * t : 128 * t + 128]


def backward(orb, w, field, gather, cas, occupied, i, j, s, p):
    columns = [w[p, pl.ds(pl.multiple_of(s * LINES + 72 * x, 8), 72), :] for x in range(9)]
    half = jnp.dot(
        cas[...], jnp.concatenate(columns, axis=1).astype(BF16), preferred_element_type=F32
    )
    lines = jnp.concatenate([half[:, 128 * x : 128 * x + 128] for x in range(9)], axis=0).astype(BF16)
    rows = [lines[ROWS * t : min(ROWS * t + ROWS, LINES)] for t in range(7)]
    parts = []
    for t in range(3):
        h = jnp.dot(
            jnp.concatenate(rows[2 * t : 2 * t + 2], axis=1), gather[t], preferred_element_type=F32
        )
        parts.append((h[:, 0:128], h[:, 128:256]))
    h = jnp.dot(rows[6], gather[3, 0:128, 0:128], preferred_element_type=F32)
    h = jnp.concatenate([h, jnp.zeros((7 * ROWS - LINES, 128), F32)], axis=0)
    potential = jnp.concatenate(
        [parts[0][0], parts[0][1] + parts[1][0], parts[1][1] + parts[2][0], parts[2][1] + h], axis=1
    )
    for target, source, other in ((i, j, False), (j, i, True)):
        weight = occupied[source, 0:1, :]
        if other:
            weight = weight * jnp.where(i == j, 0.0, 1.0)
        field[target] += (orb[source // 2, s, source % 2].astype(F32) * weight) * potential


def pack(value, occupation):
    lines = jnp.concatenate([value[x] for x in range(9)], axis=0)
    blocks = [lines[ROWS * t : ROWS * t + ROWS] for t in range(6)]
    blocks.append(jnp.concatenate([lines[6 * ROWS :], jnp.zeros((7 * ROWS - LINES, N), F32)], axis=0))
    whole = jnp.full((ROWS, LANES - 7 * N), occupation, F32)
    high = whole.astype(BF16).astype(F32)
    lane = lax.broadcasted_iota(jnp.int32, whole.shape, 1)
    blocks.append(jnp.where(lane == 0, high, jnp.where(lane == 1, whole - high, 0.0)))
    return jnp.concatenate(blocks, axis=1).astype(BF16)


def kernel(
    mine, occupation, spread, cas, gather, coulomb_hbm, out,
    orb, w, field, part, land_half, land_ring, land_x, land_turn, coulomb, occupied, send_sem, recv_sem, copy_sem,
):
    me = Place()
    started = []

    def start(source, target, index, device):
        copy = pltpu.make_async_remote_copy(
            src_ref=source,
            dst_ref=target,
            send_sem=send_sem.at[index],
            recv_sem=recv_sem.at[index],
            device_id=device,
            device_id_type=MESH,
        )
        copy.start()
        started.append(copy)
        return copy

    barrier = pltpu.get_barrier_semaphore()
    for device in me.partners():
        pl.semaphore_signal(barrier, inc=1, device_id=device, device_id_type=MESH)
    table = pltpu.make_async_copy(coulomb_hbm, coulomb, copy_sem)
    table.start()
    for o in range(2):
        orb[0, me.slab, o] = pack(mine[o], occupation[o])
    pl.semaphore_wait(barrier, len(me.partners()))

    row = (0, 0, me.row_slab, me.row_x, me.row_ring)
    col = (1, 14, me.col_slab, me.col_x, me.col_ring)
    sides = (col, row)

    def own(side, o):
        ab, base, slab, x, ring = side
        piece = orb.at[ab, slab(0, 0), o]
        return [start(piece, piece, base + 3 * o + n, device) for n, device in enumerate((x, *ring))]

    def pass_x(side, o):
        ab, base, slab, _, ring = side
        piece = orb.at[ab, slab(0, 1), o]
        return [start(piece, piece, base + 6 + 2 * o + n, ring[n]) for n in range(2)]

    def pass_far(side, line, n):
        ab, base, slab, _, ring = side
        piece = orb.at[ab, slab((3, 1)[n], line), n]
        return start(piece, piece, base + 10 + 2 * line + n, ring[n])

    turned = [start(orb.at[0, me.slab, o], orb.at[1, me.slab, o], 28 + o, me.turn) for o in range(2)]
    row_own = [own(row, o) for o in range(2)]
    row_x, col_x, col_own, far = [], [], [], []
    for o in range(2):
        row_own[o][0].wait_recv()
        row_x.append(pass_x(row, o))
    turned[0].wait_recv()
    col_own.append(own(col, 0))
    row_own[0][1].wait_recv()
    far.append(pass_far(row, 0, 0))
    turned[1].wait_recv()
    col_own.append(own(col, 1))
    row_own[1][2].wait_recv()
    far.append(pass_far(row, 0, 1))
    for o in range(2):
        col_own[o][0].wait_recv()
        col_x.append(pass_x(col, o))
    for n in range(2):
        row_x[n][n].wait_recv()
        far.append(pass_far(row, 1, n))
    for n in range(2):
        col_own[n][1 + n].wait_recv()
        far.append(pass_far(col, 0, n))
    for n in range(2):
        col_x[n][n].wait_recv()
        far.append(pass_far(col, 1, n))
    for n in range(2):
        row_own[n][2 - n].wait_recv()
        row_x[n][1 - n].wait_recv()
        col_own[n][2 - n].wait_recv()
        col_x[n][1 - n].wait_recv()

    def slab_at(steps, t):
        step = steps[0]
        for n in range(1, len(steps)):
            reached = (t // 2 + 4 - n) // 4
            step = step + (steps[n] - steps[n - 1]) * reached
        return 2 * ((me.z + step) % 4) + t % 2

    def spectra(pairs, steps):
        def body(t, _):
            s = slab_at(steps, t)
            for p in pairs:
                i, j = me.pair(p)
                forward(orb, w, spread, cas, i, j, s, p)
            return 0

        lax.fori_loop(0, 2 * len(steps), body, 0)

    on_diagonal = me.diagonal == 1
    off_diagonal = me.diagonal == 0
    pl.when(off_diagonal)(lambda: spectra(range(4), me.way_in[0:2]))
    for copy in far[:4]:
        copy.wait_recv()
    pl.when(on_diagonal)(lambda: spectra(range(3), me.way_in))
    for copy in far[4:]:
        copy.wait_recv()
    pl.when(off_diagonal)(lambda: spectra(range(4), me.way_in[2:4]))
    pl.when(on_diagonal)(lambda: spectra(range(3, 5), me.way_in))

    for q in range(4):
        terms = orb[q // 2, me.slab, q % 2, 0:16, 384:512].astype(F32)[0:8]
        occupied[q] = jnp.broadcast_to(terms[:, 120:121] + terms[:, 121:122], (8, LANES))
    table.wait()

    def solve(t, _):
        middle(w, cas, coulomb, t // (N // BLOCK), t % (N // BLOCK) * BLOCK)
        return 0

    lax.fori_loop(0, (4 + me.diagonal) * (N // BLOCK), solve, 0)

    def fields(steps):
        def body(t, _):
            s = slab_at(steps, t)
            field[...] = jnp.zeros_like(field)

            def pairs(count):
                for p in range(count):
                    i, j = me.pair(p)
                    backward(orb, w, field, gather, cas, occupied, i, j, s, p)

            pl.when(off_diagonal)(lambda: pairs(4))
            pl.when(on_diagonal)(lambda: pairs(5))
            for o in range(4):
                part[o // 2, s, o % 2] = field[o].astype(BF16)
            return 0

        lax.fori_loop(0, 2 * len(steps), body, 0)

    def add(*values):
        return sum((value.astype(F32) for value in values[1:]), values[0].astype(F32))

    far = {}

    def send_far(side):
        ab, base, slab, _, ring = side
        for line in (1, 0):
            for n in range(2):
                source = part.at[ab, slab(2, line), n]
                far[ab, line, n] = start(source, land_half.at[ab, n, line], 30 + base + 2 * line + n, ring[n])

    near = {}

    def send_near(side, line, o, n):
        ab, base, slab, _, ring = side
        s = slab((1, 3)[n], line)
        if o == n:
            far[ab, line, n].wait_recv()
            part[ab, s, o] = add(part[ab, s, o], land_half[ab, n, line]).astype(BF16)
        index = 34 + base + 4 * line + 2 * o + n
        near[ab, line, o, n] = start(part.at[ab, s, o], land_ring.at[ab, n, line, o], index, ring[n])

    across = {}

    def send_across(side, o):
        ab, base, slab, x, _ = side
        s = slab(0, 1)
        for n in range(2):
            near[ab, 1, o, n].wait_recv()
        part[ab, s, o] = add(part[ab, s, o], land_ring[ab, 0, 1, o], land_ring[ab, 1, 1, o]).astype(BF16)
        across[ab, o] = start(part.at[ab, s, o], land_x.at[ab, o], 42 + base + o, x)

    def total(side, o):
        ab, _, slab, _, _ = side
        for n in range(2):
            near[ab, 0, o, n].wait_recv()
        across[ab, o].wait_recv()
        return add(part[ab, slab(0, 0), o], land_ring[ab, 0, 0, o], land_ring[ab, 1, 0, o], land_x[ab, o])

    fields(me.way_out[0:1])
    send_far(col)
    fields(me.way_out[1:2])
    send_far(row)
    fields(me.way_out[2:4])
    for line in (1, 0):
        for o in range(2):
            for side in sides:
                send_near(side, line, o, 1 - o)
        for o in range(2):
            for side in sides:
                send_near(side, line, o, o)
    for o in range(2):
        for side in sides:
            send_across(side, o)
    returned = []
    for o in range(2):
        part[1, me.col_slab(0, 0), o] = total(col, o).astype(BF16)
        returned.append(start(part.at[1, me.col_slab(0, 0), o], land_turn.at[o], 58 + o, me.back))
    for o in range(2):
        field[o] = total(row, o)
    for o in range(2):
        returned[o].wait_recv()
        whole = field[o] + land_turn[o].astype(F32)
        blocks = [whole[:, 72 * t : 72 * t + 72] for t in range(7)]
        for x in range(9):
            out[o, x] = lines_of(blocks, 72 * x, 72)
    for copy in started:
        copy.wait_send()


def on_device(orbitals, occupation):
    vmem = pl.BlockSpec(memory_space=pltpu.VMEM)
    piece = (ROWS, LANES)
    return pl.pallas_call(
        kernel,
        out_shape=jax.ShapeDtypeStruct(orbitals.shape, F32),
        in_specs=[vmem, pl.BlockSpec(memory_space=pltpu.SMEM), vmem, vmem, vmem, pl.BlockSpec(memory_space=pl.ANY)],
        out_specs=vmem,
        scratch_shapes=[
            pltpu.VMEM((2, 8, 2, *piece), BF16),
            pltpu.VMEM((5, N * N, 128), F32),
            pltpu.VMEM((4, *piece), F32),
            pltpu.VMEM((2, 8, 2, *piece), BF16),
            pltpu.VMEM((2, 2, 2, *piece), BF16),
            pltpu.VMEM((2, 2, 2, 2, *piece), BF16),
            pltpu.VMEM((2, 2, *piece), BF16),
            pltpu.VMEM((2, *piece), BF16),
            pltpu.VMEM((N, N, 128), F32),
            pltpu.VMEM((4, 8, LANES), F32),
            pltpu.SemaphoreType.DMA((60,)),
            pltpu.SemaphoreType.DMA((60,)),
            pltpu.SemaphoreType.DMA,
        ],
        compiler_params=pltpu.CompilerParams(
            collective_id=0, has_side_effects=True, vmem_limit_bytes=56 * 2**20
        ),
        name="exchange",
    )(orbitals, occupation, *tables())


def solution(mesh):
    return jax.shard_map(
        on_device,
        mesh=mesh,
        in_specs=(jax.sharding.PartitionSpec("band", "slab", None, None), jax.sharding.PartitionSpec("band")),
        out_specs=jax.sharding.PartitionSpec("band", "slab", None, None),
        check_vma=False,
    )
```

```python
import math

import jax
import jax.numpy as jnp
import numpy as np
from jax import lax
from jax.experimental import pallas as pl
from jax.experimental.pallas import tpu as pltpu

N = 72
BOX_LENGTH = 37.25
ROWS, LANES, LINES = 96, 512, 648
F32, BF16 = jnp.float32, jnp.bfloat16
MESH = pl.DeviceIdType.MESH
BLOCK = 36


def tables():
    positions = np.arange(N)
    angles = (positions[:, None] * positions[None, :] % N) * (2.0 * math.pi / N)
    cas = np.cos(angles) + np.sin(angles)
    spread = np.zeros((4, 256, 256), np.float32)
    gather = np.zeros((4, 256, 256), np.float32)
    for block in range(7):
        window, lane = block // 2, 72 * block - 128 * (block // 2)
        column = 128 * (block % 2)
        spread[window, lane : lane + 72, column : column + 72] = cas
        gather[window, column : column + 72, lane : lane + 72] = cas
    squares = np.where(positions < N // 2, positions, positions - N).astype(np.float64) ** 2
    summed = squares[:, None, None] + squares[None, :, None] + squares[None, None, :]
    scale = 4.0 * math.pi / (2.0 * math.pi / BOX_LENGTH) ** 2 * (-1.0 / math.sqrt(32.0) / N**3)
    coulomb = np.zeros((N, N, 128), np.float32)
    coulomb[:, :, :N] = np.where(summed > 0, scale / np.where(summed > 0, summed, 1.0), 0.0)
    short = lambda value: jnp.asarray(value, F32).astype(BF16)
    return short(spread), short(cas), short(gather), jnp.asarray(coulomb)


class Place:
    def __init__(self):
        band, slab = lax.axis_index("band"), lax.axis_index("slab")
        xh, y, k = band // 8, band // 2 % 4, band % 2
        z, xl = slab // 2, slab % 2
        self.slab, self.z, self.y, self.k = slab, z, y, k
        group = xh * 4 + y
        w = (xh + xl) % 2
        column = w * 4 + z

        def swapped(of, against):
            return (of - against + 8) // 8

        kk = (k + swapped(group, column)) % 2
        far = group - column + 8
        self.diagonal = (far // 8) * ((16 - far) // 8)

        def member(xh2, xl2, y2):
            core = (kk + swapped(xh2 * 4 + y2, column)) % 2
            return (xh2 * 8 + y2 * 2 + core, 2 * z + xl2)

        self.row_x = (band, 2 * z + 1 - xl)
        self.row_ring = ((band, 2 * ((z + 1) % 4) + xl), (band, 2 * ((z + 3) % 4) + xl))
        self.col_x = member(1 - xh, 1 - xl, y)
        self.col_ring = (member(xh, xl, (y + 1) % 4), member(xh, xl, (y + 3) % 4))
        xh2 = (xh + xl + 1) % 2
        y2 = (2 * y - z + 4) % 4
        core = (k + swapped(xh2 * 4 + y2, group)) % 2
        self.turn = (xh2 * 8 + y2 * 2 + core, 2 * y + 1 - xl)
        self.back = (w * 8 + z * 2 + kk, 2 * ((2 * z - y + 4) % 4) + 1 - xl)
        self.row_slab = lambda step, line: 2 * ((z + step) % 4) + (1 - xl if line else xl)
        self.col_slab = lambda step, line: 2 * ((2 * z - y - step + 8) % 4) + (xl if line else 1 - xl)
        d = (z - y + 4) % 4
        half, last, some = d // 2, d // 3, (d + 2) // 3
        self.way_in = (half - last, 1 + 2 * half, 2 - 2 * half + last, 3 - half)
        self.way_out = ((d + 2) % 4, 1 + some, 3 - 3 * some + half - last, d + half - last)

    def partners(self):
        return (self.row_x, *self.row_ring, self.col_x, *self.col_ring, self.turn, self.back)


def lines_of(blocks, first, count):
    pieces = []
    while count:
        block, row = first // ROWS, first % ROWS
        size = min(count, ROWS - row)
        pieces.append(blocks[block][row : row + size])
        first, count = first + size, count - size
    return pieces[0] if len(pieces) == 1 else jnp.concatenate(pieces, axis=0)


def forward(orb, w, spread, cas, units):
    densities = [orb[i // 2, s, i % 2] * orb[j // 2, s, j % 2] for i, j, s, _ in units]

    def stacked(first, last, table):
        rows = jnp.concatenate([density[:, first:last] for density in densities], axis=0)
        return jnp.dot(rows, table, preferred_element_type=F32)

    windows = [stacked(128 * t, 128 * t + 256, spread[t]) for t in range(3)]
    last = stacked(384, 512, spread[3, 0:128, 0:128])
    for n, (_, _, s, p) in enumerate(units):
        rows = slice(ROWS * n, ROWS * n + ROWS)
        blocks = [window[rows, 128 * t : 128 * t + 128] for window in windows for t in range(2)]
        blocks.append(last[rows])
        columns = [lines_of(blocks, 72 * x, 72) for x in range(9)]
        planes = jnp.dot(
            cas[...], jnp.concatenate(columns, axis=1).astype(BF16), preferred_element_type=F32
        )
        for x in range(9):
            w[p, pl.ds(pl.multiple_of(s * LINES + 72 * x, 8), 72), :] = planes[:, 128 * x : 128 * x + 128]


def middle(w, cas, coulomb, p, b):
    rows = [w[p, pl.ds(b + t, 72, stride=72), :] for t in range(BLOCK)]
    spectrum = jnp.dot(
        cas[...], jnp.concatenate(rows, axis=1).astype(BF16), preferred_element_type=F32
    )
    filtered = [spectrum[:, 128 * t : 128 * t + 128] * coulomb[b + t] for t in range(BLOCK)]
    back = jnp.dot(
        cas[...], jnp.concatenate(filtered, axis=1).astype(BF16), preferred_element_type=F32
    )
    for t in range(BLOCK):
        w[p, pl.ds(b + t, 72, stride=72), :] = back[:, 128 * t : 128 * t + 128]


def backward(w, gather, cas, units):
    lines = []
    for s, p in units:
        columns = [w[p, pl.ds(pl.multiple_of(s * LINES + 72 * x, 8), 72), :] for x in range(9)]
        half = jnp.dot(
            cas[...], jnp.concatenate(columns, axis=1).astype(BF16), preferred_element_type=F32
        )
        rows = [half[:, 128 * x : 128 * x + 128] for x in range(9)]
        rows.append(jnp.zeros((7 * ROWS - LINES, 128), F32))
        lines.append(jnp.concatenate(rows, axis=0).astype(BF16))
    windows = []
    for t in range(3):
        first = 2 * t * ROWS
        rows = [
            jnp.concatenate([line[first : first + ROWS], line[first + ROWS : first + 2 * ROWS]], axis=1)
            for line in lines
        ]
        windows.append(jnp.dot(jnp.concatenate(rows, axis=0), gather[t], preferred_element_type=F32))
    rows = jnp.concatenate([line[6 * ROWS :] for line in lines], axis=0)
    last = jnp.dot(rows, gather[3, 0:128, 0:128], preferred_element_type=F32)
    potentials = []
    for n in range(len(units)):
        rows = slice(ROWS * n, ROWS * n + ROWS)
        a, b, c = (window[rows] for window in windows)
        potentials.append(
            jnp.concatenate(
                [a[:, 0:128], a[:, 128:] + b[:, 0:128], b[:, 128:] + c[:, 0:128], c[:, 128:] + last[rows]],
                axis=1,
            )
        )
    return potentials


def pack(value, occupation):
    lines = jnp.concatenate([value[x] for x in range(9)], axis=0)
    blocks = [lines[ROWS * t : ROWS * t + ROWS] for t in range(6)]
    blocks.append(jnp.concatenate([lines[6 * ROWS :], jnp.zeros((7 * ROWS - LINES, N), F32)], axis=0))
    whole = jnp.full((ROWS, LANES - 7 * N), occupation, F32)
    high = whole.astype(BF16).astype(F32)
    lane = lax.broadcasted_iota(jnp.int32, whole.shape, 1)
    blocks.append(jnp.where(lane == 0, high, jnp.where(lane == 1, whole - high, 0.0)))
    return jnp.concatenate(blocks, axis=1).astype(BF16)


def kernel(
    mine, occupation, spread, cas, gather, coulomb_hbm, out,
    orb, w, acc, part, land_half, land_ring, land_x, land_turn, coulomb, occupied, send_sem, recv_sem, copy_sem,
):
    me = Place()
    started = []

    def start(source, target, index, device):
        copy = pltpu.make_async_remote_copy(
            src_ref=source,
            dst_ref=target,
            send_sem=send_sem.at[index],
            recv_sem=recv_sem.at[index],
            device_id=device,
            device_id_type=MESH,
        )
        copy.start()
        started.append(copy)
        return copy

    barrier = pltpu.get_barrier_semaphore()
    for device in me.partners():
        pl.semaphore_signal(barrier, inc=1, device_id=device, device_id_type=MESH)
    table = pltpu.make_async_copy(coulomb_hbm, coulomb, copy_sem)
    table.start()
    for o in range(2):
        orb[0, me.slab, o] = pack(mine[o], occupation[o])
    pl.semaphore_wait(barrier, len(me.partners()))

    row = (0, 0, me.row_slab, me.row_x, me.row_ring)
    col = (1, 14, me.col_slab, me.col_x, me.col_ring)
    sides = (col, row)

    def own(side, o):
        ab, base, slab, x, ring = side
        piece = orb.at[ab, slab(0, 0), o]
        return [start(piece, piece, base + 3 * o + n, device) for n, device in enumerate((x, *ring))]

    def pass_x(side, o):
        ab, base, slab, _, ring = side
        piece = orb.at[ab, slab(0, 1), o]
        return [start(piece, piece, base + 6 + 2 * o + n, ring[n]) for n in range(2)]

    def pass_far(side, line, n):
        ab, base, slab, _, ring = side
        piece = orb.at[ab, slab((3, 1)[n], line), n]
        return start(piece, piece, base + 10 + 2 * line + n, ring[n])

    turned = [start(orb.at[0, me.slab, o], orb.at[1, me.slab, o], 28 + o, me.turn) for o in range(2)]
    row_own = [own(row, o) for o in range(2)]
    row_x, col_x, col_own, row_far, col_far = [], [], [], [], [[], []]
    for o in range(2):
        row_own[o][0].wait_recv()
        row_x.append(pass_x(row, o))
    turned[0].wait_recv()
    col_own.append(own(col, 0))
    row_own[0][1].wait_recv()
    row_far.append(pass_far(row, 0, 0))
    turned[1].wait_recv()
    col_own.append(own(col, 1))
    row_own[1][2].wait_recv()
    row_far.append(pass_far(row, 0, 1))
    col_own[0][0].wait_recv()
    col_x.append(pass_x(col, 0))
    col_own[0][1].wait_recv()
    col_far[0].append(pass_far(col, 0, 0))
    for n in range(2):
        row_x[n][n].wait_recv()
        row_far.append(pass_far(row, 1, n))
    col_own[1][0].wait_recv()
    col_x.append(pass_x(col, 1))
    col_x[0][0].wait_recv()
    col_far[0].append(pass_far(col, 1, 0))
    col_own[1][2].wait_recv()
    col_far[1].append(pass_far(col, 0, 1))
    for n in range(2):
        row_own[n][2 - n].wait_recv()
        row_x[n][1 - n].wait_recv()
    col_own[0][2].wait_recv()
    col_x[0][1].wait_recv()

    k, d = me.k, me.diagonal
    on_diagonal, off_diagonal = d == 1, d == 0

    def step_at(steps, t):
        step = steps[0]
        for n in range(1, len(steps)):
            step = step + (steps[n] - steps[n - 1]) * ((t + len(steps) - n) // len(steps))
        return step

    def slabs_at(step):
        return [2 * ((me.z + step) % 4) + line for line in range(2)]

    def over(steps, group, body):
        firsts = [steps[n::group] for n in range(group)]

        def run(t, _):
            body([slab for own_steps in firsts for slab in slabs_at(step_at(own_steps, t))])
            return 0

        lax.fori_loop(0, len(steps) // group, run, 0)

    def spectra(pairs, steps, group=1):
        over(
            steps,
            group,
            lambda slabs: forward(
                orb, w, spread, cas, [(i, j, s, p) for s in slabs for p, (i, j) in pairs]
            ),
        )

    def solve(count):
        def body(t, _):
            middle(w, cas, coulomb, t // (N // BLOCK), t % (N // BLOCK) * BLOCK)
            return 0

        lax.fori_loop(0, count * (N // BLOCK), body, 0)

    def weighed(q, s, factor=None):
        weight = occupied[q, 0:1, :]
        if factor is not None:
            weight = weight * factor
        return orb[q // 2, s, q % 2].astype(F32) * weight

    def add(*values):
        return sum((value.astype(F32) for value in values[1:]), values[0].astype(F32))

    far, near, across, returned = {}, {}, {}, {}

    def send_far(side, o):
        ab, base, slab, _, ring = side
        for line in (1, 0):
            source = part.at[ab, slab(2, line), o]
            far[ab, line, o] = start(source, land_half.at[ab, o, line], 30 + base + 2 * line + o, ring[o])

    def send_near(side, o, n):
        ab, base, slab, _, ring = side
        for line in (1, 0):
            s = slab((1, 3)[n], line)
            if o == n:
                far[ab, line, n].wait_recv()
                part[ab, s, o] = add(part[ab, s, o], land_half[ab, n, line]).astype(BF16)
            index = 34 + base + 4 * line + 2 * o + n
            near[ab, line, o, n] = start(part.at[ab, s, o], land_ring.at[ab, n, line, o], index, ring[n])

    def send_across(side, o):
        ab, base, slab, x, _ = side
        s = slab(0, 1)
        for n in range(2):
            near[ab, 1, o, n].wait_recv()
        part[ab, s, o] = add(part[ab, s, o], land_ring[ab, 0, 1, o], land_ring[ab, 1, 1, o]).astype(BF16)
        across[ab, o] = start(part.at[ab, s, o], land_x.at[ab, o], 42 + base + o, x)

    def total(side, o):
        ab, _, slab, _, _ = side
        for n in range(2):
            near[ab, 0, o, n].wait_recv()
        across[ab, o].wait_recv()
        return add(part[ab, slab(0, 0), o], land_ring[ab, 0, 0, o], land_ring[ab, 1, 0, o], land_x[ab, o])

    def send_back(o):
        s = me.col_slab(0, 0)
        part[1, s, o] = total(col, o).astype(BF16)
        returned[o] = start(part.at[1, s, o], land_turn.at[o], 58 + o, me.back)

    pl.when(off_diagonal)(lambda: spectra(((0, (0, 2)), (1, (1, 2))), me.way_in[0:2]))
    for copy in row_far:
        copy.wait_recv()
    pl.when(on_diagonal)(lambda: spectra(((1, (0, 0)), (2, (0, 1))), me.way_in))
    col_x[1][1].wait_recv()
    col_far[1].append(pass_far(col, 1, 1))
    for copy in col_far[0]:
        copy.wait_recv()
    pl.when(off_diagonal)(lambda: spectra(((0, (0, 2)), (1, (1, 2))), me.way_in[2:4]))
    pl.when(on_diagonal)(lambda: spectra(((0, (k, 2)),), me.way_in, 2))
    table.wait()
    solve(2 + d)

    def weigh(q):
        terms = orb[q // 2, me.slab, q % 2, 0:16, 384:512].astype(F32)[0:8]
        occupied[q] = jnp.broadcast_to(terms[:, 120:121] + terms[:, 121:122], (8, LANES))

    for q in range(3):
        weigh(q)

    def first_off(slabs):
        v = backward(w, gather, cas, [(s, p) for s in slabs for p in range(2)])
        for n, s in enumerate(slabs):
            v0, v1 = v[2 * n : 2 * n + 2]
            acc[0, s] = weighed(2, s) * v0
            acc[1, s] = weighed(2, s) * v1
            acc[3, s] = jnp.zeros((ROWS, LANES), F32)
            part[1, s, 0] = (weighed(0, s) * v0 + weighed(1, s) * v1).astype(BF16)

    def first_on(slabs):
        v = backward(w, gather, cas, [(s, p) for s in slabs for p in range(3)])
        for n, s in enumerate(slabs):
            v0, v1, v2 = v[3 * n : 3 * n + 3]
            acc[0, s] = weighed(0, s) * v1 + weighed(1, s) * v2
            acc[1, s] = weighed(0, s) * v2
            acc[k, s] += weighed(2, s) * v0
            acc[3, s] = jnp.zeros((ROWS, LANES), F32)
            part[1, s, 0] = (weighed(k, s) * v0).astype(BF16)

    def first(steps):
        pl.when(off_diagonal)(lambda: over(steps, 1, first_off))
        pl.when(on_diagonal)(lambda: over(steps, 1, first_on))

    first(me.way_out[0:1])
    send_far(col, 0)
    first(me.way_out[1:4])
    send_near(col, 0, 1)

    def later(i, j, factor, steps, done):
        def body(slabs):
            for s, v in zip(slabs, backward(w, gather, cas, [(s, 0) for s in slabs])):
                acc[i, s] += weighed(j, s) * v
                acc[j, s] += weighed(i, s, factor) * v
                for q in done:
                    part[q // 2, s, q % 2] = acc[q, s].astype(BF16)

        over(steps, 2, body)

    col_own[1][1].wait_recv()
    col_x[1][0].wait_recv()
    for copy in col_far[1]:
        copy.wait_recv()
    weigh(3)
    i, j = d * (1 - k), 3 - 2 * d * (1 - k)
    factor = 1.0 - (d * (1 - k)).astype(F32)
    spectra(((0, (i, j)),), (2, 1, 3, 0), 2)
    solve(1)
    send_near(col, 0, 0)
    later(i, j, factor, (2, 1), (0,))
    send_far(row, 0)
    later(i, j, factor, (3, 0), (0,))
    send_near(row, 0, 1)

    j = 3 - 2 * d * k
    factor = 1.0 - (d * k).astype(F32)
    spectra(((0, (1, j)),), (2, 1, 3, 0), 2)
    solve(1)
    send_across(col, 0)
    later(1, j, factor, me.way_out[0:2], (1, 3))
    send_far(col, 1)
    send_far(row, 1)
    later(1, j, factor, me.way_out[2:4], (1, 3))
    send_near(col, 1, 0)
    send_near(row, 1, 0)
    send_near(row, 0, 0)
    send_back(0)
    send_near(col, 1, 1)
    send_near(row, 1, 1)
    send_across(row, 0)
    send_across(col, 1)
    send_across(row, 1)
    send_back(1)
    for o in range(2):
        acc[o, 0] = total(row, o)
    for o in range(2):
        returned[o].wait_recv()
        whole = acc[o, 0] + land_turn[o].astype(F32)
        blocks = [whole[:, 72 * t : 72 * t + 72] for t in range(7)]
        for x in range(9):
            out[o, x] = lines_of(blocks, 72 * x, 72)
    for copy in started:
        copy.wait_send()


def on_device(orbitals, occupation):
    vmem = pl.BlockSpec(memory_space=pltpu.VMEM)
    piece = (ROWS, LANES)
    return pl.pallas_call(
        kernel,
        out_shape=jax.ShapeDtypeStruct(orbitals.shape, F32),
        in_specs=[vmem, pl.BlockSpec(memory_space=pltpu.SMEM), vmem, vmem, vmem, pl.BlockSpec(memory_space=pl.ANY)],
        out_specs=vmem,
        scratch_shapes=[
            pltpu.VMEM((2, 8, 2, *piece), BF16),
            pltpu.VMEM((3, N * N, 128), F32),
            pltpu.VMEM((4, 8, *piece), F32),
            pltpu.VMEM((2, 8, 2, *piece), BF16),
            pltpu.VMEM((2, 2, 2, *piece), BF16),
            pltpu.VMEM((2, 2, 2, 2, *piece), BF16),
            pltpu.VMEM((2, 2, *piece), BF16),
            pltpu.VMEM((2, *piece), BF16),
            pltpu.VMEM((N, N, 128), F32),
            pltpu.VMEM((4, 8, LANES), F32),
            pltpu.SemaphoreType.DMA((60,)),
            pltpu.SemaphoreType.DMA((60,)),
            pltpu.SemaphoreType.DMA,
        ],
        compiler_params=pltpu.CompilerParams(
            collective_id=0, has_side_effects=True, vmem_limit_bytes=56 * 2**20
        ),
        name="exchange",
    )(orbitals, occupation, *tables())


def solution(mesh):
    return jax.shard_map(
        on_device,
        mesh=mesh,
        in_specs=(jax.sharding.PartitionSpec("band", "slab", None, None), jax.sharding.PartitionSpec("band")),
        out_specs=jax.sharding.PartitionSpec("band", "slab", None, None),
        check_vma=False,
    )
```

```python
import math

import jax
import jax.numpy as jnp
import numpy as np
from jax import lax
from jax.experimental import pallas as pl
from jax.experimental.pallas import tpu as pltpu

N = 72
BOX_LENGTH = 37.25
ROWS, LANES, LINES = 96, 512, 648
F32, BF16 = jnp.float32, jnp.bfloat16
MESH = pl.DeviceIdType.MESH
BLOCK = 36


def tables():
    positions = np.arange(N)
    angles = (positions[:, None] * positions[None, :] % N) * (2.0 * math.pi / N)
    cas = np.cos(angles) + np.sin(angles)
    spread = np.zeros((4, 256, 256), np.float32)
    gather = np.zeros((4, 256, 256), np.float32)
    for block in range(7):
        window, lane = block // 2, 72 * block - 128 * (block // 2)
        column = 128 * (block % 2)
        spread[window, lane : lane + 72, column : column + 72] = cas
        gather[window, column : column + 72, lane : lane + 72] = cas
    squares = np.where(positions < N // 2, positions, positions - N).astype(np.float64) ** 2
    summed = squares[:, None, None] + squares[None, :, None] + squares[None, None, :]
    scale = 4.0 * math.pi / (2.0 * math.pi / BOX_LENGTH) ** 2 * (-1.0 / math.sqrt(32.0) / N**3)
    coulomb = np.zeros((N, N, 128), np.float32)
    coulomb[:, :, :N] = np.where(summed > 0, scale / np.where(summed > 0, summed, 1.0), 0.0)
    short = lambda value: jnp.asarray(value, F32).astype(BF16)
    return short(spread), short(cas), short(gather), jnp.asarray(coulomb)


class Place:
    def __init__(self):
        band, slab = lax.axis_index("band"), lax.axis_index("slab")
        xh, y, k = band // 8, band // 2 % 4, band % 2
        z, xl = slab // 2, slab % 2
        self.slab, self.z, self.y, self.k = slab, z, y, k
        group = xh * 4 + y
        w = (xh + xl) % 2
        column = w * 4 + z

        def swapped(of, against):
            return (of - against + 8) // 8

        kk = (k + swapped(group, column)) % 2
        far = group - column + 8
        self.diagonal = (far // 8) * ((16 - far) // 8)

        def member(xh2, xl2, y2):
            core = (kk + swapped(xh2 * 4 + y2, column)) % 2
            return (xh2 * 8 + y2 * 2 + core, 2 * z + xl2)

        self.row_x = (band, 2 * z + 1 - xl)
        self.row_ring = ((band, 2 * ((z + 1) % 4) + xl), (band, 2 * ((z + 3) % 4) + xl))
        self.col_x = member(1 - xh, 1 - xl, y)
        self.col_ring = (member(xh, xl, (y + 1) % 4), member(xh, xl, (y + 3) % 4))
        xh2 = (xh + xl + 1) % 2
        y2 = (2 * y - z + 4) % 4
        core = (k + swapped(xh2 * 4 + y2, group)) % 2
        self.turn = (xh2 * 8 + y2 * 2 + core, 2 * y + 1 - xl)
        self.back = (w * 8 + z * 2 + kk, 2 * ((2 * z - y + 4) % 4) + 1 - xl)
        self.row_slab = lambda step, line: 2 * ((z + step) % 4) + (1 - xl if line else xl)
        self.col_slab = lambda step, line: 2 * ((2 * z - y - step + 8) % 4) + (xl if line else 1 - xl)
        d = (z - y + 4) % 4
        half, last, some = d // 2, d // 3, (d + 2) // 3
        self.way_in = (half - last, 1 + 2 * half, 2 - 2 * half + last, 3 - half)
        self.way_out = ((d + 2) % 4, 1 + some, 3 - 3 * some + half - last, d + half - last)

    def partners(self):
        return (self.row_x, *self.row_ring, self.col_x, *self.col_ring, self.turn, self.back)


def lines_of(blocks, first, count):
    pieces = []
    while count:
        block, row = first // ROWS, first % ROWS
        size = min(count, ROWS - row)
        pieces.append(blocks[block][row : row + size])
        first, count = first + size, count - size
    return pieces[0] if len(pieces) == 1 else jnp.concatenate(pieces, axis=0)


def forward(orb, w, spread, cas, units):
    densities = [orb[i // 2, s, i % 2] * orb[j // 2, s, j % 2] for i, j, s, _ in units]

    def stacked(first, last, table):
        rows = jnp.concatenate([density[:, first:last] for density in densities], axis=0)
        return jnp.dot(rows, table, preferred_element_type=F32)

    windows = [stacked(128 * t, 128 * t + 256, spread[t]) for t in range(3)]
    last = stacked(384, 512, spread[3, 0:128, 0:128])
    for n, (_, _, s, p) in enumerate(units):
        rows = slice(ROWS * n, ROWS * n + ROWS)
        blocks = [window[rows, 128 * t : 128 * t + 128] for window in windows for t in range(2)]
        blocks.append(last[rows])
        columns = [lines_of(blocks, 72 * x, 72) for x in range(9)]
        planes = jnp.dot(
            cas[...], jnp.concatenate(columns, axis=1).astype(BF16), preferred_element_type=F32
        )
        for x in range(9):
            w[p, pl.ds(pl.multiple_of(s * LINES + 72 * x, 8), 72), :] = planes[:, 128 * x : 128 * x + 128]


def middle(w, cas, coulomb, p, b):
    rows = [w[p, pl.ds(b + t, 72, stride=72), :] for t in range(BLOCK)]
    spectrum = jnp.dot(
        cas[...], jnp.concatenate(rows, axis=1).astype(BF16), preferred_element_type=F32
    )
    filtered = [spectrum[:, 128 * t : 128 * t + 128] * coulomb[b + t] for t in range(BLOCK)]
    back = jnp.dot(
        cas[...], jnp.concatenate(filtered, axis=1).astype(BF16), preferred_element_type=F32
    )
    for t in range(BLOCK):
        w[p, pl.ds(b + t, 72, stride=72), :] = back[:, 128 * t : 128 * t + 128]


def backward(w, gather, cas, units):
    lines = []
    for s, p in units:
        columns = [w[p, pl.ds(pl.multiple_of(s * LINES + 72 * x, 8), 72), :] for x in range(9)]
        half = jnp.dot(
            cas[...], jnp.concatenate(columns, axis=1).astype(BF16), preferred_element_type=F32
        )
        rows = [half[:, 128 * x : 128 * x + 128] for x in range(9)]
        rows.append(jnp.zeros((7 * ROWS - LINES, 128), F32))
        lines.append(jnp.concatenate(rows, axis=0).astype(BF16))
    windows = []
    for t in range(3):
        first = 2 * t * ROWS
        rows = [
            jnp.concatenate([line[first : first + ROWS], line[first + ROWS : first + 2 * ROWS]], axis=1)
            for line in lines
        ]
        windows.append(jnp.dot(jnp.concatenate(rows, axis=0), gather[t], preferred_element_type=F32))
    rows = jnp.concatenate([line[6 * ROWS :] for line in lines], axis=0)
    last = jnp.dot(rows, gather[3, 0:128, 0:128], preferred_element_type=F32)
    potentials = []
    for n in range(len(units)):
        rows = slice(ROWS * n, ROWS * n + ROWS)
        a, b, c = (window[rows] for window in windows)
        potentials.append(
            jnp.concatenate(
                [a[:, 0:128], a[:, 128:] + b[:, 0:128], b[:, 128:] + c[:, 0:128], c[:, 128:] + last[rows]],
                axis=1,
            )
        )
    return potentials


def pack(value, occupation):
    lines = jnp.concatenate([value[x] for x in range(9)], axis=0)
    blocks = [lines[ROWS * t : ROWS * t + ROWS] for t in range(6)]
    blocks.append(jnp.concatenate([lines[6 * ROWS :], jnp.zeros((7 * ROWS - LINES, N), F32)], axis=0))
    whole = jnp.full((ROWS, LANES - 7 * N), occupation, F32)
    high = whole.astype(BF16).astype(F32)
    lane = lax.broadcasted_iota(jnp.int32, whole.shape, 1)
    blocks.append(jnp.where(lane == 0, high, jnp.where(lane == 1, whole - high, 0.0)))
    return jnp.concatenate(blocks, axis=1).astype(BF16)


def kernel(
    mine, occupation, spread, cas, gather, coulomb_hbm, out,
    orb, w, acc, part, land_half, land_ring, land_x, land_turn, coulomb, occupied, send_sem, recv_sem, copy_sem,
):
    me = Place()
    started = []

    def start(source, target, device):
        index = len(started)
        copy = pltpu.make_async_remote_copy(
            src_ref=source,
            dst_ref=target,
            send_sem=send_sem.at[index],
            recv_sem=recv_sem.at[index],
            device_id=device,
            device_id_type=MESH,
        )
        copy.start()
        started.append(copy)
        return copy

    barrier = pltpu.get_barrier_semaphore()
    for device in me.partners():
        pl.semaphore_signal(barrier, inc=1, device_id=device, device_id_type=MESH)
    table = pltpu.make_async_copy(coulomb_hbm, coulomb, copy_sem)
    table.start()
    for o in range(2):
        orb[0, me.slab, o] = pack(mine[o], occupation[o])
    pl.semaphore_wait(barrier, len(me.partners()))

    row = (0, me.row_slab, me.row_x, me.row_ring)
    col = (1, me.col_slab, me.col_x, me.col_ring)
    sides = (col, row)

    def own(side, o):
        ab, slab, x, ring = side
        piece = orb.at[ab, slab(0, 0), o]
        return [start(piece, piece, device) for device in (x, *ring)]

    def pass_x(side, o):
        ab, slab, _, ring = side
        piece = orb.at[ab, slab(0, 1), o]
        return [start(piece, piece, ring[n]) for n in range(2)]

    def pass_far(side, line, n):
        ab, slab, _, ring = side
        piece = orb.at[ab, slab((3, 1)[n], line), n]
        return start(piece, piece, ring[n])

    def slab_at(steps, t):
        step = steps[0]
        for n in range(1, len(steps)):
            reached = (t // 2 + 4 - n) // 4
            step = step + (steps[n] - steps[n - 1]) * reached
        return 2 * ((me.z + step) % 4) + t % 2

    k = me.k
    on_diagonal, off_diagonal = me.diagonal == 1, me.diagonal == 0
    block = tuple((p, (p // 2, 2 + p % 2)) for p in range(4))

    def spectra(pairs, steps):
        def body(t, _):
            s = slab_at(steps, t)
            forward(orb, w, spread, cas, [(i, j, s, p) for p, (i, j) in pairs])
            return 0

        lax.fori_loop(0, 2 * len(steps), body, 0)

    def solve(first, count):
        def body(t, _):
            middle(w, cas, coulomb, first + t // (N // BLOCK), t % (N // BLOCK) * BLOCK)
            return 0

        lax.fori_loop(0, count * (N // BLOCK), body, 0)

    inner = ((2, (0, 0)), (3, (0, 1)), (4, (1, 1)))

    def inner_spectra(step):
        pl.when(on_diagonal)(lambda: spectra(inner, (step,)))

    turned = [start(orb.at[0, me.slab, o], orb.at[1, me.slab, o], me.turn) for o in range(2)]
    row_own = [own(row, o) for o in range(2)]
    row_x, col_x, col_own, far = [], [], [], []
    for o in range(2):
        row_own[o][0].wait_recv()
        row_x.append(pass_x(row, o))
    turned[0].wait_recv()
    col_own.append(own(col, 0))
    row_own[0][1].wait_recv()
    far.append(pass_far(row, 0, 0))
    turned[1].wait_recv()
    col_own.append(own(col, 1))
    row_own[1][2].wait_recv()
    far.append(pass_far(row, 0, 1))
    inner_spectra(0)
    for o in range(2):
        col_own[o][0].wait_recv()
        col_x.append(pass_x(col, o))
    for n in range(2):
        row_x[n][n].wait_recv()
        far.append(pass_far(row, 1, n))
    for n in range(2):
        row_own[n][2 - n].wait_recv()
        row_x[n][1 - n].wait_recv()
    inner_spectra(1)
    for n in range(2):
        col_own[n][1 + n].wait_recv()
        far.append(pass_far(col, 0, n))
    inner_spectra(3)
    for n in range(2):
        col_x[n][n].wait_recv()
        far.append(pass_far(col, 1, n))
    for copy in far[:4]:
        copy.wait_recv()
    table.wait()
    inner_spectra(2)
    pl.when(on_diagonal)(lambda: solve(2, 3))
    for n in range(2):
        col_own[n][2 - n].wait_recv()
        col_x[n][1 - n].wait_recv()
    across_pairs = ((0, (0, 2 + k)), (1, (1, 3 - k)))
    pl.when(on_diagonal)(lambda: spectra(across_pairs, me.way_in[0:2]))
    pl.when(off_diagonal)(lambda: spectra(block, me.way_in[0:2]))
    for copy in far[4:]:
        copy.wait_recv()
    pl.when(off_diagonal)(lambda: spectra(block, me.way_in[2:4]))
    pl.when(on_diagonal)(lambda: spectra(across_pairs, me.way_in[2:4]))

    for q in range(4):
        terms = orb[q // 2, me.slab, q % 2, 0:16, 384:512].astype(F32)[0:8]
        occupied[q] = jnp.broadcast_to(terms[:, 120:121] + terms[:, 121:122], (8, LANES))
    solve(0, 4 - 2 * me.diagonal)

    def weighed(q, s):
        return orb[q // 2, s, q % 2].astype(F32) * occupied[q, 0:1, :]

    def block_fields(s):
        v = backward(w, gather, cas, [(s, p) for p in range(4)])
        for o in range(2):
            part[0, s, o] = (weighed(2, s) * v[2 * o] + weighed(3, s) * v[2 * o + 1]).astype(BF16)
            part[1, s, o] = (weighed(0, s) * v[o] + weighed(1, s) * v[2 + o]).astype(BF16)

    def diagonal_fields(s):
        v = backward(w, gather, cas, [(s, p) for p in range(5)])
        part[0, s, 0] = (weighed(0, s) * v[2] + weighed(1, s) * v[3] + weighed(2 + k, s) * v[0]).astype(BF16)
        part[0, s, 1] = (weighed(0, s) * v[3] + weighed(1, s) * v[4] + weighed(3 - k, s) * v[1]).astype(BF16)
        part[1, s, k] = (weighed(0, s) * v[0]).astype(BF16)
        part[1, s, 1 - k] = (weighed(1, s) * v[1]).astype(BF16)

    def fields(steps):
        def body(t, _):
            s = slab_at(steps, t)
            pl.when(off_diagonal)(lambda: block_fields(s))
            pl.when(on_diagonal)(lambda: diagonal_fields(s))
            return 0

        lax.fori_loop(0, 2 * len(steps), body, 0)

    def add(*values):
        return sum((value.astype(F32) for value in values[1:]), values[0].astype(F32))

    half = (slice(0, ROWS // 2), slice(ROWS // 2, ROWS))
    far, near, across, returned = {}, {}, {}, {}

    def send_far(side, o):
        ab, slab, _, ring = side
        for line in (1, 0):
            for h in range(2):
                source = part.at[ab, slab(2, line), o, half[h]]
                far[ab, line, o, h] = start(source, land_half.at[ab, o, line, h], ring[h])

    def send_near(side, o, line, passing):
        ab, slab, _, ring = side
        for h in range(2):
            n = h if passing else 1 - h
            s = slab((1, 3)[n], line)
            if passing:
                far[ab, line, o, h].wait_recv()
                part[ab, s, o, half[h]] = add(part[ab, s, o, half[h]], land_half[ab, o, line, h]).astype(BF16)
            source, target = part.at[ab, s, o, half[h]], land_ring.at[ab, n, line, o, half[h]]
            near[ab, line, o, h, n] = start(source, target, ring[n])

    def send_across(side, o):
        ab, slab, x, _ = side
        s = slab(0, 1)
        for h in range(2):
            for n in range(2):
                near[ab, 1, o, h, n].wait_recv()
            landed = [land_ring[ab, n, 1, o, half[h]] for n in range(2)]
            part[ab, s, o, half[h]] = add(part[ab, s, o, half[h]], *landed).astype(BF16)
            across[ab, o, h] = start(part.at[ab, s, o, half[h]], land_x.at[ab, o, half[h]], x)

    def total(side, o, h):
        ab, slab, _, _ = side
        for n in range(2):
            near[ab, 0, o, h, n].wait_recv()
        across[ab, o, h].wait_recv()
        landed = [land_ring[ab, n, 0, o, half[h]] for n in range(2)]
        return add(part[ab, slab(0, 0), o, half[h]], *landed, land_x[ab, o, half[h]])

    def send_back(o):
        s = me.col_slab(0, 0)
        for h in range(2):
            part[1, s, o, half[h]] = total(col, o, h).astype(BF16)
            returned[o, h] = start(part.at[1, s, o, half[h]], land_turn.at[o, half[h]], me.back)

    fields(me.way_out[0:1])
    send_far(col, 0)
    send_far(col, 1)
    fields(me.way_out[1:2])
    send_far(row, 0)
    send_far(row, 1)
    fields(me.way_out[2:4])
    for side in sides:
        send_near(side, 0, 1, False)
    for side in sides:
        send_near(side, 0, 0, False)
    for line in (1, 0):
        for side in sides:
            send_near(side, 0, line, True)
    for line in (1, 0):
        for side in sides:
            send_near(side, 1, line, False)
    for line in (1, 0):
        for side in sides:
            send_near(side, 1, line, True)
    send_across(col, 0)
    send_across(row, 0)
    send_back(0)
    send_across(col, 1)
    send_across(row, 1)
    send_back(1)
    for o in range(2):
        for h in range(2):
            acc[o, half[h]] = total(row, o, h)
    for o in range(2):
        for h in range(2):
            returned[o, h].wait_recv()
        whole = acc[o] + land_turn[o].astype(F32)
        blocks = [whole[:, 72 * t : 72 * t + 72] for t in range(7)]
        for x in range(9):
            out[o, x] = lines_of(blocks, 72 * x, 72)
    for copy in started:
        copy.wait_send()


def on_device(orbitals, occupation):
    vmem = pl.BlockSpec(memory_space=pltpu.VMEM)
    piece = (ROWS, LANES)
    return pl.pallas_call(
        kernel,
        out_shape=jax.ShapeDtypeStruct(orbitals.shape, F32),
        in_specs=[vmem, pl.BlockSpec(memory_space=pltpu.SMEM), vmem, vmem, vmem, pl.BlockSpec(memory_space=pl.ANY)],
        out_specs=vmem,
        scratch_shapes=[
            pltpu.VMEM((2, 8, 2, *piece), BF16),
            pltpu.VMEM((5, N * N, 128), F32),
            pltpu.VMEM((2, *piece), F32),
            pltpu.VMEM((2, 8, 2, *piece), BF16),
            pltpu.VMEM((2, 2, 2, 2, ROWS // 2, LANES), BF16),
            pltpu.VMEM((2, 2, 2, 2, *piece), BF16),
            pltpu.VMEM((2, 2, *piece), BF16),
            pltpu.VMEM((2, *piece), BF16),
            pltpu.VMEM((N, N, 128), F32),
            pltpu.VMEM((4, 8, LANES), F32),
            pltpu.SemaphoreType.DMA((90,)),
            pltpu.SemaphoreType.DMA((90,)),
            pltpu.SemaphoreType.DMA,
        ],
        compiler_params=pltpu.CompilerParams(
            collective_id=0, has_side_effects=True, vmem_limit_bytes=56 * 2**20
        ),
        name="exchange",
    )(orbitals, occupation, *tables())


def solution(mesh):
    return jax.shard_map(
        on_device,
        mesh=mesh,
        in_specs=(jax.sharding.PartitionSpec("band", "slab", None, None), jax.sharding.PartitionSpec("band")),
        out_specs=jax.sharding.PartitionSpec("band", "slab", None, None),
        check_vma=False,
    )
```
